32 devices in a mesh: sy: 4 (over y, x), sz: 8 (over z, core).
Axes of the slice: x: 2, y: 2, z: 4, core: 2. Of those that a mesh axis runs over, the one named last changes fastest.
Arguments:
- labels: int32 [16, 256, 256], P(None, 'sy', 'sz'), may hold values from 0 to 3
- wall_dist: bfloat16 [16, 256, 256], P(None, 'sy', 'sz'), may hold values from -5 to 5
- material_table: bfloat16 [4, 16], replicated, may hold values from -4 to 4
- dist_weight: bfloat16 [16], replicated, may hold values from -4 to 4
- conv_weight: bfloat16 [27, 16, 16], replicated, may hold values from -0.3125 to 0.3125
- down_weight: bfloat16 [8, 64, 16], replicated, may hold values from -0.5 to 0.5
- mix_weight: bfloat16 [64, 128, 128], P('sz'), may hold values from -0.5 to 0.5
- cotangent: bfloat16 [64, 8, 128, 128], P('sz', None, 'sy'), may hold values from -6 to 6
Outputs:
- mid_features: bfloat16 [64, 8, 128, 128], P('sz', None, 'sy')
- mix_grad: float32 [64, 128, 128], P('sz', 'sy')
- down_grad: float32 [8, 64, 16], replicated
- conv_grad: float32 [27, 16, 16], replicated
The draws below stay inside these ranges and needn't reach their ends.
All inputs are finite; a program needn't handle non-finite values.
Results may differ from the reference program's by a relative error of at most 0.0084.
Values may be sent and summed in bfloat16 or wider, within the bound.
A program may use at most 192 MiB of HBM per device.

```python
import math
import jax
import jax.numpy as jnp
from jax import lax

C1 = 16
C2 = 64
NMAT = 4
XD = 16
NY = 256
NZ = 256
X2 = 8
NY2 = 128
NZ2 = 128


def touch_ends(values, stream_key, smallest, largest):
    dims = values.shape
    index_at = [jax.random.randint(jax.random.fold_in(stream_key, axis), (), 0, dims[axis]) for axis in range(len(dims))]
    values = values.at[tuple(index_at)].set(smallest)
    longest = dims.index(max(dims))
    index_at[longest] = (index_at[longest] + 1) % dims[longest]
    return values.at[tuple(index_at)].set(largest)


def steps_of(key, shape, cuts, least, top_value):
    def one(axis_at, parts):
        draws = jax.random.uniform(jax.random.fold_in(jax.random.fold_in(key, 6), axis_at), (parts,), jnp.float32, least / len(cuts), top_value / len(cuts))
        return jnp.repeat(jnp.exp(draws), shape[axis_at] // parts).reshape((-1,) + (1,) * (len(shape) - axis_at - 1))

    loudness = one(*cuts[0])
    for cut in cuts[1:]:
        loudness = loudness * one(*cut)
    return loudness


def gaussian(rng, extent, width, bound, pieces=(), kind=jnp.bfloat16):
    entries = jax.random.normal(rng, extent, jnp.float32) * width
    if len(pieces) > 0:
        entries = steps_of(rng, extent, pieces, -0.22, 0.18) * entries
    return jnp.clip(entries, min=-bound, max=bound).astype(kind)


def setup_inputs(seed: int = 0) -> dict:
    arg_keys = jax.random.split(jax.random.key(seed), 9)
    return {
        "labels": touch_ends(jax.random.randint(arg_keys[0], (XD, NY, NZ), 0, NMAT), jax.random.fold_in(arg_keys[0], 1), 0, NMAT - 1).astype(jnp.int32),
        "wall_dist": gaussian(arg_keys[1], (XD, NY, NZ), 1.0, 5.0, ((1, 4), (2, 8))),
        "material_table": gaussian(arg_keys[2], (NMAT, C1), 1.0, 4.0),
        "dist_weight": gaussian(arg_keys[3], (C1,), 1.0, 4.0),
        "conv_weight": gaussian(arg_keys[4], (27, C1, C1), (27 * C1) ** -0.5, 0.3125),
        "down_weight": gaussian(arg_keys[5], (8, C2, C1), (8 * C1) ** -0.5, 0.5),
        "mix_weight": gaussian(arg_keys[6], (C2, NZ2, NZ2), NZ2 ** -0.5, 0.5, ((0, 8),)),
        "cotangent": gaussian(arg_keys[7], (C2, X2, NY2, NZ2), 1.0, 6.0, ((0, 8), (2, 4))),
    }


def silu_slope(values):
    sigma = jax.nn.sigmoid(values)
    return sigma * (1.0 + values * (1.0 - sigma))

def conv_first(embedded_f, kernel_taps):
    kernel = jnp.transpose(kernel_taps.reshape(3, 3, 3, C1, C1), (3, 4, 0, 1, 2))
    result = lax.conv_general_dilated(embedded_f[None], kernel, (1, 1, 1), ((1, 1), (1, 1), (1, 1)), dimension_numbers=('NCDHW', 'OIDHW', 'NCDHW'), precision=lax.Precision.HIGHEST)
    return result[0]

def reference(labels, wall_dist, material_table, dist_weight, conv_weight, down_weight, mix_weight, cotangent):
    looked = jnp.transpose(material_table.astype(jnp.float32)[labels], (3, 0, 1, 2))
    embedded = (looked + dist_weight.astype(jnp.float32)[:, None, None, None] * wall_dist.astype(jnp.float32)[None]).astype(jnp.bfloat16)
    embedded_f = embedded.astype(jnp.float32)
    pre_act, pullback = jax.vjp(lambda kernel_taps: conv_first(embedded_f, kernel_taps), conv_weight.astype(jnp.float32))
    hidden = jax.nn.silu(pre_act).astype(jnp.bfloat16)
    hidden_r = hidden.astype(jnp.float32).reshape(C1, X2, 2, NY2, 2, NZ2, 2)
    down_r = down_weight.astype(jnp.float32).reshape(2, 2, 2, C2, C1)
    coarse = jnp.einsum('abcoi,ixaybzc->oxyz', down_r, hidden_r).astype(jnp.bfloat16)
    coarse_f = coarse.astype(jnp.float32)
    mix_f = mix_weight.astype(jnp.float32)
    mixed_pre = jnp.einsum('czw,cxyw->cxyz', mix_f, coarse_f)
    mid_features = jax.nn.silu(mixed_pre).astype(jnp.bfloat16)
    mixed_grad = (cotangent.astype(jnp.float32) * silu_slope(mixed_pre)).astype(jnp.bfloat16)
    mixed_grad_f = mixed_grad.astype(jnp.float32)
    mix_grad = jnp.einsum('cxyz,cxyw->czw', mixed_grad_f, coarse_f) / math.sqrt(X2 * NY2)
    coarse_grad = jnp.einsum('czw,cxyz->cxyw', mix_f, mixed_grad_f).astype(jnp.bfloat16)
    coarse_grad_f = coarse_grad.astype(jnp.float32)
    down_grad = jnp.einsum('oxyz,ixaybzc->abcoi', coarse_grad_f, hidden_r).reshape(8, C2, C1) / math.sqrt(X2 * NY2 * NZ2)
    hidden_grad = jnp.einsum('abcoi,oxyz->ixaybzc', down_r, coarse_grad_f).reshape(C1, XD, NY, NZ)
    pre_grad = (hidden_grad * silu_slope(pre_act)).astype(jnp.bfloat16)
    conv_grad = pullback(pre_grad.astype(jnp.float32))[0] / math.sqrt(XD * NY * NZ)
    return (mid_features, mix_grad, down_grad, conv_grad)
```

```python
import math

import jax
import jax.numpy as jnp
import numpy as np
from jax import lax
from jax.sharding import PartitionSpec as P


def extended(value, sides, width):
    for axis, dim in sides:
        size, length = (lax.axis_size(axis), value.shape[dim])
        up = [(i, (i + 1) % size) for i in range(size - 1)]
        down = [(j, i) for i, j in up]
        last = lax.slice_in_dim(value, length - width, length, axis=dim)
        first = lax.slice_in_dim(value, 0, width, axis=dim)
        before = lax.ppermute(last, axis, up)
        after = lax.ppermute(first, axis, down)
        value = jnp.concatenate([before, value, after], axis=dim)
    return value


def silu_slope(values):
    sigma = jax.nn.sigmoid(values)
    return sigma * (1.0 + values * (1.0 - sigma))


def window_picks(half):
    picks = np.zeros((2 * half + 2, 4 * half), np.float32)
    for u in range(4):
        for h in range(half):
            picks[2 * h + u, u * half + h] = 1.0
    return jnp.asarray(picks, jnp.bfloat16)


def dot(spec, left, right):
    return jnp.einsum(spec, left, right, preferred_element_type=jnp.float32)


def per_device(
    labels, wall_dist, material_table, dist_weight, conv_weight, down_weight, mix_weight, cotangent
):
    depth, rows_y, rows_z = labels.shape
    materials, channels = material_table.shape
    wide_channels = down_weight.shape[1]
    count_y = lax.axis_size("sy")
    count_z = lax.axis_size("sz")
    half_x, half_y, half_z = depth // 2, rows_y // 2, rows_z // 2
    plane = half_x * half_y
    cells = half_z * plane
    corners = [(a, b, c) for a in range(2) for b in range(2) for c in range(2)]

    taps = jnp.transpose(conv_weight, (0, 2, 1)).reshape(3, 3, 3, channels, channels)
    conv_matrix = jnp.concatenate(
        [jnp.pad(taps, ((a, 1 - a), (b, 1 - b), (c, 1 - c), (0, 0), (0, 0))) for a, b, c in corners],
        axis=4,
    ).reshape(64 * channels, 8 * channels)
    down_matrix = jnp.concatenate([down_weight[t] for t in range(8)], axis=1)

    stacked = jnp.stack([(labels + 1).astype(jnp.bfloat16), wall_dist])
    widened = extended(stacked, (("sy", 2), ("sz", 3)), 1)
    windows = dot("txyz,yq->txzq", widened, window_picks(half_y)).astype(jnp.bfloat16)
    windows = dot("txzq,zr->txrq", windows, window_picks(half_z)).astype(jnp.bfloat16)
    windows = jnp.pad(windows, ((0, 0), (1, 1), (0, 0), (0, 0)))
    windows = windows.reshape(2, half_x + 1, 2, 4, half_z, 4, half_y)
    windows = jnp.stack(
        [windows[:, w // 2 : w // 2 + half_x, w % 2] for w in range(4)], axis=1
    )
    windows = jnp.transpose(windows, (0, 1, 5, 3, 4, 2, 6)).reshape(2, 64, 1, cells)
    kinds = windows[0].astype(jnp.float32)
    distance = windows[1].astype(jnp.float32)
    total = dist_weight.astype(jnp.float32)[None, :, None] * distance
    for entry in range(materials):
        column = material_table[entry].astype(jnp.float32)[None, :, None]
        total = total + jnp.where(kinds == entry + 1, column, 0.0)
    patches = total.astype(jnp.bfloat16).reshape(64 * channels, cells)

    pre_act = dot("km,kn->mn", conv_matrix, patches)
    hidden = jax.nn.silu(pre_act).astype(jnp.bfloat16)
    coarse = dot("om,mn->on", down_matrix, hidden).astype(jnp.bfloat16)
    coarse = coarse.reshape(wide_channels, half_z, plane)
    channel_coarse = lax.all_to_all(coarse, "sz", split_axis=0, concat_axis=1, tiled=True)
    mixed_pre = dot("czw,cwp->cpz", mix_weight, channel_coarse)
    mid_features = jax.nn.silu(mixed_pre).astype(jnp.bfloat16).reshape(cotangent.shape)
    gradient = cotangent.astype(jnp.float32).reshape(mixed_pre.shape)
    mixed_grad = (gradient * silu_slope(mixed_pre)).astype(jnp.bfloat16)
    channel_grad = dot("czw,cpz->cwp", mix_weight, mixed_grad).astype(jnp.bfloat16)
    coarse_grad = lax.all_to_all(channel_grad, "sz", split_axis=1, concat_axis=0, tiled=True)
    coarse_grad = coarse_grad.reshape(wide_channels, cells)
    mix_partial = dot("cpz,cwp->czw", mixed_grad, channel_coarse)
    mix_grad = lax.psum_scatter(mix_partial, "sy", scatter_dimension=1, tiled=True) / math.sqrt(
        plane * count_y
    )

    down_partial = dot("on,mn->om", coarse_grad, hidden)
    hidden_grad = dot("om,on->mn", down_matrix, coarse_grad)
    pre_grad = (hidden_grad * silu_slope(pre_act)).astype(jnp.bfloat16)
    correlated = dot("kn,mn->km", patches, pre_grad).reshape(4, 4, 4, channels, 8 * channels)
    conv_partial = sum(
        correlated[a : a + 3, b : b + 3, c : c + 3, :, t * channels : (t + 1) * channels]
        for t, (a, b, c) in enumerate(corners)
    )
    width = 8 * channels
    parts = jnp.concatenate([down_partial, conv_partial.reshape(-1, width)], axis=0)
    parts = lax.psum(parts, ("sy", "sz"))
    cells_fine = depth * rows_y * count_y * rows_z * count_z
    cells_coarse = cells_fine // 8
    down_total = parts[:wide_channels].reshape(wide_channels, 8, channels)
    conv_total = parts[wide_channels:].reshape(27, channels, channels)
    down_grad = jnp.transpose(down_total, (1, 0, 2)) / math.sqrt(cells_coarse)
    conv_grad = jnp.transpose(conv_total, (0, 2, 1)) / math.sqrt(cells_fine)
    return (mid_features, mix_grad, down_grad, conv_grad)


def solution(mesh):
    in_specs = (
        P(None, "sy", "sz"),
        P(None, "sy", "sz"),
        P(),
        P(),
        P(),
        P(),
        P("sz", None, None),
        P("sz", None, "sy", None),
    )
    out_specs = (P("sz", None, "sy", None), P("sz", "sy", None), P(), P())
    return jax.shard_map(
        per_device, mesh=mesh, in_specs=in_specs, out_specs=out_specs, check_vma=False
    )
```

```python
import math

import jax
import jax.numpy as jnp
import numpy as np
from jax import lax
from jax.sharding import PartitionSpec as P


def extended(value, sides, width):
    for axis, dim in sides:
        size, length = (lax.axis_size(axis), value.shape[dim])
        up = [(i, (i + 1) % size) for i in range(size - 1)]
        down = [(j, i) for i, j in up]
        last = lax.slice_in_dim(value, length - width, length, axis=dim)
        first = lax.slice_in_dim(value, 0, width, axis=dim)
        before = lax.ppermute(last, axis, up)
        after = lax.ppermute(first, axis, down)
        value = jnp.concatenate([before, value, after], axis=dim)
    return value


def silu_slope(values):
    sigma = jax.nn.sigmoid(values)
    return sigma * (1.0 + values * (1.0 - sigma))


def window_picks(half):
    picks = np.zeros((2 * half + 2, 4 * half), np.float32)
    for u in range(4):
        for h in range(half):
            picks[2 * h + u, u * half + h] = 1.0
    return jnp.asarray(picks, jnp.bfloat16)


def dot(spec, left, right):
    return jnp.einsum(spec, left, right, preferred_element_type=jnp.float32)


def per_device(
    labels, wall_dist, material_table, dist_weight, conv_weight, down_weight, mix_weight, cotangent
):
    depth, rows_y, rows_z = labels.shape
    materials, channels = material_table.shape
    wide_channels = down_weight.shape[1]
    count_y = lax.axis_size("sy")
    count_z = lax.axis_size("sz")
    half_x, half_y, half_z = depth // 2, rows_y // 2, rows_z // 2
    plane = half_x * half_y
    cells = half_z * plane
    corners = [(a, b, c) for a in range(2) for b in range(2) for c in range(2)]

    taps = jnp.transpose(conv_weight, (0, 2, 1)).reshape(3, 3, 3, channels, channels)
    conv_matrix = jnp.concatenate(
        [jnp.pad(taps, ((a, 1 - a), (b, 1 - b), (c, 1 - c), (0, 0), (0, 0))) for a, b, c in corners],
        axis=4,
    ).reshape(64 * channels, 8 * channels)
    down_matrix = jnp.concatenate([down_weight[t] for t in range(8)], axis=1)

    stacked = jnp.stack([(labels + 1).astype(jnp.bfloat16), wall_dist])
    widened = extended(stacked, (("sy", 2), ("sz", 3)), 1)
    windows = dot("txyz,yq->txzq", widened, window_picks(half_y)).astype(jnp.bfloat16)
    windows = dot("txzq,zr->txrq", windows, window_picks(half_z)).astype(jnp.bfloat16)
    windows = jnp.pad(windows, ((0, 0), (1, 1), (0, 0), (0, 0)))
    windows = windows.reshape(2, half_x + 1, 2, 4, half_z, 4, half_y)
    windows = jnp.stack(
        [windows[:, w // 2 : w // 2 + half_x, w % 2] for w in range(4)], axis=1
    )
    windows = jnp.transpose(windows, (0, 1, 5, 3, 4, 2, 6)).reshape(2, 64, cells)
    features = [(windows[0] == entry + 1).astype(jnp.bfloat16) for entry in range(materials)]
    features = jnp.concatenate(features + [windows[1]], axis=0)
    own = jnp.arange(64)[:, None] == (jnp.arange(64 * channels) // channels)[None, :]
    table = jnp.concatenate([material_table, dist_weight[None]], axis=0)
    table = jnp.tile(table, (1, 64))
    table = jnp.concatenate(
        [jnp.where(own, table[f][None], jnp.zeros((), table.dtype)) for f in range(materials + 1)],
        axis=0,
    )
    patches = dot("fm,fn->mn", table, features).astype(jnp.bfloat16)

    pre_act = dot("km,kn->mn", conv_matrix, patches)
    hidden = jax.nn.silu(pre_act).astype(jnp.bfloat16)
    coarse = dot("om,mn->on", down_matrix, hidden).astype(jnp.bfloat16)
    coarse = coarse.reshape(wide_channels, half_z, plane)
    channel_coarse = lax.all_to_all(coarse, "sz", split_axis=0, concat_axis=1, tiled=True)
    mixed_pre = dot("czw,cwp->cpz", mix_weight, channel_coarse)
    mid_features = jax.nn.silu(mixed_pre).astype(jnp.bfloat16).reshape(cotangent.shape)
    gradient = cotangent.astype(jnp.float32).reshape(mixed_pre.shape)
    mixed_grad = (gradient * silu_slope(mixed_pre)).astype(jnp.bfloat16)
    channel_grad = dot("czw,cpz->cwp", mix_weight, mixed_grad).astype(jnp.bfloat16)
    coarse_grad = lax.all_to_all(channel_grad, "sz", split_axis=1, concat_axis=0, tiled=True)
    coarse_grad = coarse_grad.reshape(wide_channels, cells)
    mix_partial = dot("cpz,cwp->czw", mixed_grad, channel_coarse)
    mix_grad = lax.psum_scatter(mix_partial, "sy", scatter_dimension=1, tiled=True) / math.sqrt(
        plane * count_y
    )

    down_partial = dot("on,mn->om", coarse_grad, hidden)
    hidden_grad = dot("om,on->mn", down_matrix, coarse_grad)
    pre_grad = (hidden_grad * silu_slope(pre_act)).astype(jnp.bfloat16)
    correlated = dot("kn,mn->km", patches, pre_grad).reshape(4, 4, 4, channels, 8 * channels)
    conv_partial = sum(
        correlated[a : a + 3, b : b + 3, c : c + 3, :, t * channels : (t + 1) * channels]
        for t, (a, b, c) in enumerate(corners)
    )
    width = 8 * channels
    parts = jnp.concatenate([down_partial, conv_partial.reshape(-1, width)], axis=0)
    parts = lax.psum(parts, ("sy", "sz"))
    cells_fine = depth * rows_y * count_y * rows_z * count_z
    cells_coarse = cells_fine // 8
    down_total = parts[:wide_channels].reshape(wide_channels, 8, channels)
    conv_total = parts[wide_channels:].reshape(27, channels, channels)
    down_grad = jnp.transpose(down_total, (1, 0, 2)) / math.sqrt(cells_coarse)
    conv_grad = jnp.transpose(conv_total, (0, 2, 1)) / math.sqrt(cells_fine)
    return (mid_features, mix_grad, down_grad, conv_grad)


def solution(mesh):
    in_specs = (
        P(None, "sy", "sz"),
        P(None, "sy", "sz"),
        P(),
        P(),
        P(),
        P(),
        P("sz", None, None),
        P("sz", None, "sy", None),
    )
    out_specs = (P("sz", None, "sy", None), P("sz", "sy", None), P(), P())
    return jax.shard_map(
        per_device, mesh=mesh, in_specs=in_specs, out_specs=out_specs, check_vma=False
    )
```

```python
import functools
import math

import jax
import jax.numpy as jnp
import numpy as np
from jax import lax
from jax.experimental import pallas as pl
from jax.experimental.pallas import tpu as pltpu
from jax.sharding import PartitionSpec as P


def extended(value, sides, width):
    for axis, dim in sides:
        size, length = (lax.axis_size(axis), value.shape[dim])
        up = [(i, (i + 1) % size) for i in range(size - 1)]
        down = [(j, i) for i, j in up]
        last = lax.slice_in_dim(value, length - width, length, axis=dim)
        first = lax.slice_in_dim(value, 0, width, axis=dim)
        before = lax.ppermute(last, axis, up)
        after = lax.ppermute(first, axis, down)
        value = jnp.concatenate([before, value, after], axis=dim)
    return value


def silu_slope(values):
    sigma = jax.nn.sigmoid(values)
    return sigma * (1.0 + values * (1.0 - sigma))


def window_picks(half):
    picks = np.zeros((2 * half + 2, 4 * half), np.float32)
    for u in range(4):
        for h in range(half):
            picks[2 * h + u, u * half + h] = 1.0
    return jnp.asarray(picks, jnp.bfloat16)


def dot(spec, left, right):
    return jnp.einsum(spec, left, right, preferred_element_type=jnp.float32)


def total_kernel(count_y, count_z, x_ref, out_ref, first, second, gathered, s1, r1, s2, r2, s3, r3):
    my_y, my_z = lax.axis_index("sy"), lax.axis_index("sz")
    peers_y = [{"sy": lax.rem(my_y + d, count_y)} for d in range(1, count_y)]
    peers_z = [{"sz": lax.rem(my_z + d, count_z)} for d in range(1, count_z)]

    def send(src, dst, send_sem, recv_sem, peer):
        copy = pltpu.make_async_remote_copy(
            src_ref=src,
            dst_ref=dst,
            send_sem=send_sem,
            recv_sem=recv_sem,
            device_id=peer,
            device_id_type=pl.DeviceIdType.MESH,
        )
        copy.start()
        return copy

    barrier = pltpu.get_barrier_semaphore()
    for peer in peers_y + peers_z:
        pl.semaphore_signal(barrier, inc=1, device_id=peer, device_id_type=pl.DeviceIdType.MESH)
    pl.semaphore_wait(barrier, count_y + count_z - 2)

    copies = [
        send(x_ref.at[peer["sz"]], first.at[d], s1.at[d], r1.at[d], peer)
        for d, peer in enumerate(peers_z)
    ]
    total = x_ref[my_z]
    for d, copy in enumerate(copies):
        copy.wait()
        total = total + first[d]
    second[my_y] = total
    copies = [
        send(second.at[my_y], second.at[my_y], s2.at[d], r2.at[d], peer)
        for d, peer in enumerate(peers_y)
    ]
    for copy in copies:
        copy.wait()
    total = second[0]
    for entry in range(1, count_y):
        total = total + second[entry]
    gathered[my_z] = total
    copies = [
        send(gathered.at[my_z], gathered.at[my_z], s3.at[d], r3.at[d], peer)
        for d, peer in enumerate(peers_z)
    ]
    for copy in copies:
        copy.wait()
    out_ref[...] = gathered[...]


def total_of(parts, count_y, count_z):
    rows, lanes = parts.shape
    chunk = -(-rows // (8 * count_z)) * 8
    padded = jnp.pad(parts, ((0, chunk * count_z - rows), (0, 0)))
    whole = (count_z, chunk, lanes)
    dma = pltpu.SemaphoreType.DMA
    summed = pl.pallas_call(
        functools.partial(total_kernel, count_y, count_z),
        out_shape=jax.ShapeDtypeStruct(whole, jnp.float32),
        in_specs=[pl.BlockSpec(memory_space=pltpu.VMEM)],
        out_specs=pl.BlockSpec(memory_space=pltpu.VMEM),
        scratch_shapes=[
            pltpu.VMEM((count_z - 1, chunk, lanes), jnp.float32),
            pltpu.VMEM((count_y, chunk, lanes), jnp.float32),
            pltpu.VMEM(whole, jnp.float32),
            dma((count_z - 1,)),
            dma((count_z - 1,)),
            dma((count_y - 1,)),
            dma((count_y - 1,)),
            dma((count_z - 1,)),
            dma((count_z - 1,)),
        ],
        compiler_params=pltpu.CompilerParams(collective_id=0, has_side_effects=True),
    )(padded.reshape(whole))
    return summed.reshape(chunk * count_z, lanes)[:rows]


def per_device(
    labels, wall_dist, material_table, dist_weight, conv_weight, down_weight, mix_weight, cotangent
):
    depth, rows_y, rows_z = labels.shape
    materials, channels = material_table.shape
    wide_channels = down_weight.shape[1]
    count_y = lax.axis_size("sy")
    count_z = lax.axis_size("sz")
    half_x, half_y, half_z = depth // 2, rows_y // 2, rows_z // 2
    plane = half_x * half_y
    cells = half_z * plane
    corners = [(a, b, c) for a in range(2) for b in range(2) for c in range(2)]

    taps = jnp.transpose(conv_weight, (0, 2, 1)).reshape(3, 3, 3, channels, channels)
    conv_matrix = jnp.concatenate(
        [jnp.pad(taps, ((a, 1 - a), (b, 1 - b), (c, 1 - c), (0, 0), (0, 0))) for a, b, c in corners],
        axis=4,
    ).reshape(64 * channels, 8 * channels)
    down_matrix = jnp.concatenate([down_weight[t] for t in range(8)], axis=1)

    stacked = jnp.stack([(labels + 1).astype(jnp.bfloat16), wall_dist])
    widened = extended(stacked, (("sy", 2), ("sz", 3)), 1)
    windows = dot("txyz,yq->txzq", widened, window_picks(half_y)).astype(jnp.bfloat16)
    windows = dot("txzq,zr->txrq", windows, window_picks(half_z)).astype(jnp.bfloat16)
    windows = jnp.pad(windows, ((0, 0), (1, 1), (0, 0), (0, 0)))
    windows = windows.reshape(2, half_x + 1, 2, 4, half_z, 4, half_y)
    windows = jnp.stack(
        [windows[:, w // 2 : w // 2 + half_x, w % 2] for w in range(4)], axis=1
    )
    windows = jnp.transpose(windows, (0, 1, 5, 3, 4, 2, 6)).reshape(2, 64, cells)
    features = [(windows[0] == entry + 1).astype(jnp.bfloat16) for entry in range(materials)]
    features = jnp.concatenate(features + [windows[1]], axis=0)
    own = jnp.arange(64)[:, None] == (jnp.arange(64 * channels) // channels)[None, :]
    table = jnp.concatenate([material_table, dist_weight[None]], axis=0)
    table = jnp.tile(table, (1, 64))
    table = jnp.concatenate(
        [jnp.where(own, table[f][None], jnp.zeros((), table.dtype)) for f in range(materials + 1)],
        axis=0,
    )
    patches = dot("fm,fn->mn", table, features).astype(jnp.bfloat16)

    pre_act = dot("km,kn->mn", conv_matrix, patches)
    hidden = jax.nn.silu(pre_act).astype(jnp.bfloat16)
    coarse = dot("om,mn->on", down_matrix, hidden).astype(jnp.bfloat16)
    coarse = coarse.reshape(wide_channels, half_z, plane)
    channel_coarse = lax.all_to_all(coarse, "sz", split_axis=0, concat_axis=1, tiled=True)
    mixed_pre = dot("czw,cwp->cpz", mix_weight, channel_coarse)
    mid_features = jax.nn.silu(mixed_pre).astype(jnp.bfloat16).reshape(cotangent.shape)
    gradient = cotangent.astype(jnp.float32).reshape(mixed_pre.shape)
    mixed_grad = (gradient * silu_slope(mixed_pre)).astype(jnp.bfloat16)
    channel_grad = dot("czw,cpz->cwp", mix_weight, mixed_grad).astype(jnp.bfloat16)
    coarse_grad = lax.all_to_all(channel_grad, "sz", split_axis=1, concat_axis=0, tiled=True)
    coarse_grad = coarse_grad.reshape(wide_channels, cells)
    mix_partial = dot("cpz,cwp->czw", mixed_grad, channel_coarse)
    mix_grad = lax.psum_scatter(mix_partial, "sy", scatter_dimension=1, tiled=True) / math.sqrt(
        plane * count_y
    )

    down_partial = dot("on,mn->om", coarse_grad, hidden)
    hidden_grad = dot("om,on->mn", down_matrix, coarse_grad)
    pre_grad = (hidden_grad * silu_slope(pre_act)).astype(jnp.bfloat16)
    correlated = dot("kn,mn->km", patches, pre_grad).reshape(4, 4, 4, channels, 8 * channels)
    conv_partial = sum(
        correlated[a : a + 3, b : b + 3, c : c + 3, :, t * channels : (t + 1) * channels]
        for t, (a, b, c) in enumerate(corners)
    )
    width = 8 * channels
    parts = jnp.concatenate([down_partial, conv_partial.reshape(-1, width)], axis=0)
    parts = total_of(parts, count_y, count_z)
    cells_fine = depth * rows_y * count_y * rows_z * count_z
    cells_coarse = cells_fine // 8
    down_total = parts[:wide_channels].reshape(wide_channels, 8, channels)
    conv_total = parts[wide_channels:].reshape(27, channels, channels)
    down_grad = jnp.transpose(down_total, (1, 0, 2)) / math.sqrt(cells_coarse)
    conv_grad = jnp.transpose(conv_total, (0, 2, 1)) / math.sqrt(cells_fine)
    return (mid_features, mix_grad, down_grad, conv_grad)


def solution(mesh):
    in_specs = (
        P(None, "sy", "sz"),
        P(None, "sy", "sz"),
        P(),
        P(),
        P(),
        P(),
        P("sz", None, None),
        P("sz", None, "sy", None),
    )
    out_specs = (P("sz", None, "sy", None), P("sz", "sy", None), P(), P())
    return jax.shard_map(
        per_device, mesh=mesh, in_specs=in_specs, out_specs=out_specs, check_vma=False
    )
```
